32 devices in a mesh: gx: 8 (over y, x, core), gy: 4 (over z).
Axes of the slice: x: 2, y: 2, z: 4, core: 2. Of those that a mesh axis runs over, the one named last changes fastest.
Arguments:
- provisional: bfloat16 [4, 8, 1024, 1024], P(None, 'gx', 'gy'), may hold values from -6 to 6
- implicit_terms: bfloat16 [4, 8, 1024, 1024], P(None, 'gx', 'gy'), may hold values from -6 to 6
- adv_speed: float32 [8, 1024], P('gx'), may hold values from 0.2 to 1.2
- reaction: float32 [8, 1024], P('gx'), may hold values from 0.1 to 2
- wall_rate: float32 [1024], replicated, may hold values from 0.05 to 20
- span_rate: float32 [1024], replicated, may hold values from 0.01 to 4
- analysis: bfloat16 [1024, 1024], replicated, may hold values from -1 to 2
- synthesis: bfloat16 [1024, 1024], replicated, may hold values from -1 to 2
Outputs:
- end_value: float32 [8, 1024, 1024], P('gx', 'gy')
The draws below stay inside these ranges and needn't reach their ends.
All inputs are finite; a program needn't handle non-finite values.
Results may differ from the reference program's by a relative error of at most 0.0063.
Values may be sent and summed in bfloat16 or wider, within the bound.
A program may use at most 64 MiB of HBM per device.

```python
import math
import jax
import jax.numpy as jnp
from jax import lax

NY = 1024
NZ = 1024
NODES = 4
NX = 8


def near_identity(key, offset_tag):
    subkey = jax.random.fold_in(key, offset_tag)
    entry_scale = 1.0 / jnp.sqrt(jnp.float32(NY))
    off_diagonal = jax.random.truncated_normal(subkey, -4.0, 4.0, (NY, NY), jnp.float32) * (0.35 * entry_scale)
    return (jnp.eye(NY, dtype=jnp.float32) + off_diagonal).astype(jnp.bfloat16)


def draw_analysis(key, part):
    return near_identity(key, 11)


def draw_synthesis(key, part):
    return near_identity(key, 23)


def shard_levels(stream_key, extent, shards, smallest, high):
    factor_of = 1.0
    for position, parts in shards:
        draws = jax.random.uniform(jax.random.fold_in(jax.random.fold_in(stream_key, 6), position), (parts,), jnp.float32, smallest / len(shards), high / len(shards))
        factor_of = factor_of * jnp.repeat(jnp.exp(draws), extent[position] // parts).reshape((-1,) + (1,) * (len(extent) - 1 - position))
    return factor_of


def bell_draw(rng, dims, width, most, split=(), kind=jnp.bfloat16):
    array = width * jax.random.normal(rng, dims, jnp.float32)
    if split:
        array = array * shard_levels(rng, dims, split, -0.22, 0.18)
    return jnp.clip(array, -most, most).astype(kind)


def setup_inputs(seed: int = 0) -> dict:
    streams_of = jax.random.split(jax.random.key(seed), 9)
    provisional = bell_draw(streams_of[0], (NODES, NX, NY, NZ), 1.0, 6.0, ((1, 8), (2, 4)))
    implicit_terms = bell_draw(streams_of[1], (NODES, NX, NY, NZ), 1.0, 6.0, ((1, 8), (2, 4)))
    adv_speed = jnp.clip(0.2 + 1 * jax.random.uniform(streams_of[2], (NX, NY), jnp.float32) ** shard_levels(streams_of[2], (NX, NY), ((0, 8),), -0.2, 0.2), 0.2, 1.2)
    reaction = jnp.clip(jnp.exp(math.log(2.0) - 2.9957323 * jax.random.uniform(streams_of[3], (NX, NY), jnp.float32) ** shard_levels(streams_of[3], (NX, NY), ((0, 8),), -0.2, 0.2)), 0.1, 2.0)
    wall_rate = jnp.clip(jnp.exp(jax.random.uniform(streams_of[4], (NY,), jnp.float32, math.log(0.05), math.log(20.0))), 0.05, 20.0)
    span_rate = jnp.clip(jnp.exp(jax.random.uniform(streams_of[5], (NZ,), jnp.float32, math.log(0.01), math.log(4.0))), 0.01, 4.0)
    analysis = draw_analysis(jax.random.fold_in(streams_of[8], 71), 0)
    synthesis = draw_synthesis(jax.random.fold_in(streams_of[8], 71), 0)
    return {"provisional": provisional, "implicit_terms": implicit_terms, "adv_speed": adv_speed, "reaction": reaction, "wall_rate": wall_rate, "span_rate": span_rate, "analysis": analysis, "synthesis": synthesis}


def spectral_weights():
    root_five = math.sqrt(5.0)
    points = [0.0, 0.5 - 0.5 / root_five, 0.5 + 0.5 / root_five, 1.0]
    gauss_offset = 1.0 / math.sqrt(3.0)
    weights = [[0.0, 0.0, 0.0, 0.0] for m in range(3)]
    for m in range(3):
        half_width = 0.5 * (points[m + 1] - points[m])
        centre = 0.5 * (points[m + 1] + points[m])
        for sign_factor in (-1.0, 1.0):
            sample = centre + half_width * sign_factor * gauss_offset
            for j in range(4):
                basis_value = 1.0
                for i in range(4):
                    if i != j:
                        basis_value = basis_value * (sample - points[i]) / (points[j] - points[i])
                weights[m][j] = weights[m][j] + half_width * basis_value
    return (points, weights)

def explicit_term(values, adv_speed, reaction):
    field_f32 = values.astype(jnp.float32)
    forward = jnp.roll(field_f32, -1, axis=0)
    behind = jnp.roll(field_f32, 1, axis=0)
    return -adv_speed[:, :, None] * (forward - behind) * 0.5 - reaction[:, :, None] * field_f32

def wall_solve(rounded, analysis, synthesis, factors):

    def one_plane(plane):
        coefficients = jnp.dot(analysis, plane, preferred_element_type=jnp.float32)
        scaled = (coefficients * factors).astype(jnp.bfloat16)
        return jnp.dot(synthesis, scaled, preferred_element_type=jnp.float32)
    return lax.map(one_plane, rounded)

def reference(provisional, implicit_terms, adv_speed, reaction, wall_rate, span_rate, analysis, synthesis):
    points, weights = spectral_weights()
    old_explicit = [explicit_term(provisional[j], adv_speed, reaction) for j in range(4)]
    current = provisional[0].astype(jnp.float32)
    new_explicit = old_explicit[0]
    for m in range(3):
        step_size = float(points[m + 1] - points[m])
        quadrature = jnp.zeros_like(current)
        for j in range(4):
            quadrature = quadrature + float(weights[m][j]) * (old_explicit[j] + implicit_terms[j].astype(jnp.float32))
        rhs = current + step_size * (new_explicit - old_explicit[m]) - step_size * implicit_terms[m + 1].astype(jnp.float32) + quadrature
        rounded = rhs.astype(jnp.bfloat16)
        factors = 1.0 / (1.0 + step_size * (wall_rate[:, None] + span_rate[None, :]))
        current = wall_solve(rounded, analysis, synthesis, factors)
        if m < 2:
            new_explicit = explicit_term(current.astype(jnp.bfloat16), adv_speed, reaction)
    return current
```

```python
import math

import jax
import jax.numpy as jnp
from jax import lax
from jax.sharding import PartitionSpec as P


def spectral_weights():
    root_five = math.sqrt(5.0)
    points = [0.0, 0.5 - 0.5 / root_five, 0.5 + 0.5 / root_five, 1.0]
    gauss_offset = 1.0 / math.sqrt(3.0)
    weights = [[0.0, 0.0, 0.0, 0.0] for m in range(3)]
    for m in range(3):
        half_width = 0.5 * (points[m + 1] - points[m])
        centre = 0.5 * (points[m + 1] + points[m])
        for sign_factor in (-1.0, 1.0):
            sample = centre + half_width * sign_factor * gauss_offset
            for j in range(4):
                basis_value = 1.0
                for i in range(4):
                    if i != j:
                        basis_value = basis_value * (sample - points[i]) / (points[j] - points[i])
                weights[m][j] = weights[m][j] + half_width * basis_value
    return (points, weights)


def shifted(cells, axis):
    count = lax.axis_size(axis)
    behind = lax.ppermute(cells, axis, [(i, (i + 1) % count) for i in range(count)])
    forward = lax.ppermute(cells, axis, [((i + 1) % count, i) for i in range(count)])
    return forward.astype(jnp.float32) - behind.astype(jnp.float32)


def per_device(
    provisional, implicit_terms, adv_speed, reaction, wall_rate, span_rate, analysis, synthesis
):
    points, weights = spectral_weights()
    steps = [float(points[m + 1] - points[m]) for m in range(3)]
    modes_dev = span_rate.shape[0] // lax.axis_size("gy")
    span_part = lax.dynamic_slice_in_dim(span_rate, lax.axis_index("gy") * modes_dev, modes_dev, 0)
    rows_dev = provisional.shape[2]
    row_start = lax.axis_index("gy") * rows_dev
    half_speed = 0.5 * adv_speed[0][:, None]
    decay = reaction[0][:, None]
    half_speed_part = lax.dynamic_slice_in_dim(half_speed, row_start, rows_dev, 0)
    decay_part = lax.dynamic_slice_in_dim(decay, row_start, rows_dev, 0)
    prov = [provisional[j, 0].astype(jnp.float32) for j in range(4)]
    impl = [implicit_terms[j, 0].astype(jnp.float32) for j in range(4)]
    known = []
    for m in range(3):
        field_weights = [weights[m][j] - (steps[m] if m == j and m > 0 else 0.0) for j in range(4)]
        impl_weights = [weights[m][j] - (steps[m] if j == m + 1 else 0.0) for j in range(4)]
        mixed = sum(float(field_weights[j]) * prov[j] for j in range(4))
        local = sum(float(impl_weights[j]) * impl[j] for j in range(4)) - decay_part * mixed
        if m == 0:
            local = local + prov[0]
        local = local - half_speed_part * shifted(mixed.astype(jnp.bfloat16), "gx")
        known.append(local.astype(jnp.bfloat16))
    known = [
        lax.all_to_all(field, "gy", split_axis=1, concat_axis=0, tiled=True) for field in known
    ]
    for m in range(3):
        rhs = known[m].astype(jnp.float32)
        if m:
            sent = current.astype(jnp.bfloat16)
            rhs = rhs + current - steps[m] * (
                decay * sent.astype(jnp.float32) + half_speed * shifted(sent, "gx")
            )
        factors = 1.0 / (1.0 + steps[m] * (wall_rate[:, None] + span_part[None, :]))
        coefficients = jnp.dot(
            analysis, rhs.astype(jnp.bfloat16), preferred_element_type=jnp.float32
        )
        scaled = (coefficients * factors).astype(jnp.bfloat16)
        current = jnp.dot(synthesis, scaled, preferred_element_type=jnp.float32)
    result = lax.all_to_all(
        current.astype(jnp.bfloat16), "gy", split_axis=0, concat_axis=1, tiled=True
    )
    return result.astype(jnp.float32)[None]


def solution(mesh):
    placed = (
        P(None, "gx", "gy", None),
        P(None, "gx", "gy", None),
        P("gx", None),
        P("gx", None),
        P(),
        P(),
        P(),
        P(),
    )
    return jax.shard_map(
        per_device, mesh=mesh, in_specs=placed, out_specs=P("gx", "gy", None), check_vma=False
    )
```

```python
import functools
import math

import jax
import jax.numpy as jnp
from jax import lax
from jax.experimental import pallas as pl
from jax.experimental.pallas import tpu as pltpu
from jax.sharding import PartitionSpec as P

TILE = 64
BLOCK = 256
PARTS = 2


def spectral_weights():
    root_five = math.sqrt(5.0)
    points = [0.0, 0.5 - 0.5 / root_five, 0.5 + 0.5 / root_five, 1.0]
    gauss_offset = 1.0 / math.sqrt(3.0)
    weights = [[0.0, 0.0, 0.0, 0.0] for m in range(3)]
    for m in range(3):
        half_width = 0.5 * (points[m + 1] - points[m])
        centre = 0.5 * (points[m + 1] + points[m])
        for sign_factor in (-1.0, 1.0):
            sample = centre + half_width * sign_factor * gauss_offset
            for j in range(4):
                basis_value = 1.0
                for i in range(4):
                    if i != j:
                        basis_value = basis_value * (sample - points[i]) / (points[j] - points[i])
                weights[m][j] = weights[m][j] + half_width * basis_value
    return (points, weights)


def sweep_kernel(
    planes,
    groups,
    parts,
    prov_hbm,
    impl_hbm,
    speed_ref,
    reaction_ref,
    wall_ref,
    span_ref,
    ana_hbm,
    syn_hbm,
    out_ref,
    prov,
    impl,
    ana,
    syn,
    cols,
    mixed,
    mixed_recv,
    local,
    known_send,
    known,
    current,
    rounded,
    scaled,
    sent,
    sent_recv,
    final,
    load_sem,
    mixed_sem,
    mixed_recv_sem,
    known_sem,
    known_recv_sem,
    sent_sem,
    sent_recv_sem,
    final_sem,
    final_recv_sem,
):
    f32, bf16 = jnp.float32, jnp.bfloat16
    rows, modes = prov.shape[1], known.shape[2]
    height = rows * groups
    width = modes // parts
    points, weights = spectral_weights()
    steps = [float(points[m + 1] - points[m]) for m in range(3)]
    gx, me = lax.axis_index("gx"), lax.axis_index("gy")
    sides = (lax.rem(gx + 1, planes), lax.rem(gx + planes - 1, planes))
    row_start = pl.multiple_of(me * rows, rows)
    order = list(range(1, groups)) + [0]

    loads = []
    for j in range(4):
        loads.append(pltpu.make_async_copy(prov_hbm.at[j, 0], prov.at[j], load_sem.at[j]))
    for j in range(4):
        loads.append(pltpu.make_async_copy(impl_hbm.at[j, 0], impl.at[j], load_sem.at[4 + j]))
    loads.append(pltpu.make_async_copy(ana_hbm, ana, load_sem.at[8]))
    loads.append(pltpu.make_async_copy(syn_hbm, syn, load_sem.at[9]))
    for load in loads:
        load.start()

    barrier = pltpu.get_barrier_semaphore()
    for side in sides:
        pl.semaphore_signal(
            barrier, inc=1, device_id=(side, me), device_id_type=pl.DeviceIdType.MESH
        )
    for s in range(1, groups):
        pl.semaphore_signal(
            barrier,
            inc=1,
            device_id=(gx, lax.rem(me + s, groups)),
            device_id_type=pl.DeviceIdType.MESH,
        )

    def over(total, tile, body):
        def step(i, carry):
            body(pl.multiple_of(i * tile, tile))
            return carry

        lax.fori_loop(0, total // tile, step, 0)

    def lanes_of(s):
        return pl.ds(pl.multiple_of(lax.rem(me + s, groups) * modes, modes), modes)

    def remote(src, dst, send, recv, where):
        return pltpu.make_async_remote_copy(
            src_ref=src,
            dst_ref=dst,
            send_sem=send,
            recv_sem=recv,
            device_id=where,
            device_id_type=pl.DeviceIdType.MESH,
        )

    for k, ref in enumerate((speed_ref, reaction_ref, wall_ref)):
        for i in range(height // 128):
            line = ref[0:1, i * 128 : (i + 1) * 128] * (0.5 if k == 0 else 1.0)
            block = jnp.broadcast_to(line, (128, 128)).T
            for lane in range(modes // 128):
                cols[k, i * 128 : (i + 1) * 128, lane * 128 : (lane + 1) * 128] = block

    def mix(m, r, lanes):
        total = None
        for j in range(4):
            weight = float(weights[m][j] - (steps[m] if m == j and m > 0 else 0.0))
            term = weight * prov[j, pl.ds(r, TILE), lanes].astype(f32)
            total = term if total is None else total + term
        return total

    def make_mixed(m, s):
        lanes = lanes_of(s)

        def body(r):
            mixed[m, s, pl.ds(r, TILE), :] = mix(m, r, lanes).astype(bf16)

        over(rows, TILE, body)

    def make_local(m, s):
        lanes = lanes_of(s)

        def body(r):
            here = pl.ds(pl.multiple_of(row_start + r, TILE), TILE)
            total = -cols[1, here, :] * mix(m, r, lanes)
            if m == 0:
                total = total + prov[0, pl.ds(r, TILE), lanes].astype(f32)
            for j in range(4):
                weight = float(weights[m][j] - (steps[m] if j == m + 1 else 0.0))
                total = total + weight * impl[j, pl.ds(r, TILE), lanes].astype(f32)
            local[m, s, pl.ds(r, TILE), :] = total

        over(rows, TILE, body)

    mixed_copies, known_copies, sent_copies, final_copies = {}, {}, {}, {}

    def send_mixed(m, s):
        for d in range(2):
            copy = remote(
                mixed.at[m, s],
                mixed_recv.at[m, d, s],
                mixed_sem.at[m, d, s],
                mixed_recv_sem.at[m, d, s],
                (sides[d], me),
            )
            copy.start()
            mixed_copies[m, d, s] = copy

    def make_known(m, s):
        for d in range(2):
            mixed_copies[m, d, s].wait_recv()

        def body(r):
            here = pl.ds(pl.multiple_of(row_start + r, TILE), TILE)
            ahead = mixed_recv[m, 1, s, pl.ds(r, TILE), :].astype(f32)
            behind = mixed_recv[m, 0, s, pl.ds(r, TILE), :].astype(f32)
            value = local[m, s, pl.ds(r, TILE), :] - cols[0, here, :] * (ahead - behind)
            if s:
                known_send[m, s - 1, pl.ds(r, TILE), :] = value.astype(bf16)
            else:
                known[m, here, :] = value.astype(bf16)

        over(rows, TILE, body)
        if s:
            copy = remote(
                known_send.at[m, s - 1],
                known.at[m, pl.ds(row_start, rows)],
                known_sem.at[m, s - 1],
                known_recv_sem.at[m, s - 1],
                (gx, lax.rem(me + s, groups)),
            )
            copy.start()
            known_copies[m, s] = copy

    def solve(m, p):
        span = span_ref[
            0:1, pl.ds(pl.multiple_of(me * modes + p * width, width), width)
        ]
        part = slice(p * width, (p + 1) * width)

        def make_rhs(r):
            here = pl.ds(r, TILE)
            rhs = known[m, here, part].astype(f32)
            if m:
                ahead = sent_recv[m - 1, 1, p, here, :].astype(f32)
                behind = sent_recv[m - 1, 0, p, here, :].astype(f32)
                own = sent[m - 1, p, here, :].astype(f32)
                rhs = (
                    rhs
                    + current[p, here, :]
                    - steps[m]
                    * (cols[1, here, part] * own + cols[0, here, part] * (ahead - behind))
                )
            rounded[p, here, :] = rhs.astype(bf16)

        over(height, TILE, make_rhs)

        def to_modes(r):
            here = pl.ds(r, BLOCK)
            factors = 1.0 / (1.0 + steps[m] * (cols[2, here, part] + span))
            coefficients = jnp.dot(ana[here, :], rounded[p], preferred_element_type=f32)
            scaled[p, here, :] = (coefficients * factors).astype(bf16)

        over(height, BLOCK, to_modes)

        def to_points(r):
            here = pl.ds(r, BLOCK)
            value = jnp.dot(syn[here, :], scaled[p], preferred_element_type=f32)
            if m < 2:
                current[p, here, :] = value
                sent[m, p, here, :] = value.astype(bf16)
            else:
                final[p, here, :] = value.astype(bf16)

        over(height, BLOCK, to_points)
        if m < 2:
            for d in range(2):
                copy = remote(
                    sent.at[m, p],
                    sent_recv.at[m, d, p],
                    sent_sem.at[m, d, p],
                    sent_recv_sem.at[m, d, p],
                    (sides[d], me),
                )
                copy.start()
                sent_copies[m, d, p] = copy
        else:
            own = pl.ds(pl.multiple_of(me * modes + p * width, width), width)
            for s in range(1, groups):
                other = lax.rem(me + s, groups)
                copy = remote(
                    final.at[p, pl.ds(pl.multiple_of(other * rows, rows), rows)],
                    out_ref.at[:, own],
                    final_sem.at[p, s - 1],
                    final_recv_sem.at[p, s - 1],
                    (gx, other),
                )
                copy.start()
                final_copies[p, s] = copy
            out_ref[:, own] = final[p, pl.ds(row_start, rows), :]

    for load in loads[:4]:
        load.wait()
    for s in order:
        make_mixed(0, s)
        if s == order[0]:
            pl.semaphore_wait(barrier, 2 + groups - 1)
        send_mixed(0, s)
    for load in loads[4:8]:
        load.wait()
    for s in order:
        make_local(0, s)
    for m in (1, 2):
        for s in order:
            make_mixed(m, s)
    for s in order:
        make_known(0, s)
    for m in (1, 2):
        for s in order:
            send_mixed(m, s)
    for m in (1, 2):
        for s in order:
            make_local(m, s)
    for load in loads[8:]:
        load.wait()
    for m in range(3):
        for s in range(1, groups):
            known_copies[m, s].wait_recv()
        for p in range(parts):
            if m:
                for d in range(2):
                    sent_copies[m - 1, d, p].wait_recv()
            solve(m, p)
        if m == 0:
            for later in (1, 2):
                for s in order:
                    make_known(later, s)
    for copy in final_copies.values():
        copy.wait_recv()
    for group in (mixed_copies, known_copies, sent_copies, final_copies):
        for copy in group.values():
            copy.wait_send()


def per_device(
    provisional, implicit_terms, adv_speed, reaction, wall_rate, span_rate, analysis, synthesis
):
    planes, groups = lax.axis_size("gx"), lax.axis_size("gy")
    rows, total = provisional.shape[2], provisional.shape[3]
    height, modes = rows * groups, total // groups
    parts = max(1, min(PARTS, modes // 128))
    width = modes // parts
    f32, bf16 = jnp.float32, jnp.bfloat16
    dma = pltpu.SemaphoreType.DMA
    vmem = pl.BlockSpec(memory_space=pltpu.VMEM)
    hbm = pl.BlockSpec(memory_space=pl.ANY)
    result = pl.pallas_call(
        functools.partial(sweep_kernel, planes, groups, parts),
        out_shape=jax.ShapeDtypeStruct((rows, total), bf16),
        in_specs=[hbm, hbm, vmem, vmem, vmem, vmem, hbm, hbm],
        out_specs=vmem,
        scratch_shapes=[
            pltpu.VMEM((4, rows, total), bf16),
            pltpu.VMEM((4, rows, total), bf16),
            pltpu.VMEM((height, height), bf16),
            pltpu.VMEM((height, height), bf16),
            pltpu.VMEM((3, height, modes), f32),
            pltpu.VMEM((3, groups, rows, modes), bf16),
            pltpu.VMEM((3, 2, groups, rows, modes), bf16),
            pltpu.VMEM((3, groups, rows, modes), f32),
            pltpu.VMEM((3, groups - 1, rows, modes), bf16),
            pltpu.VMEM((3, height, modes), bf16),
            pltpu.VMEM((parts, height, width), f32),
            pltpu.VMEM((parts, height, width), bf16),
            pltpu.VMEM((parts, height, width), bf16),
            pltpu.VMEM((2, parts, height, width), bf16),
            pltpu.VMEM((2, 2, parts, height, width), bf16),
            pltpu.VMEM((parts, height, width), bf16),
            dma((10,)),
            dma((3, 2, groups)),
            dma((3, 2, groups)),
            dma((3, groups - 1)),
            dma((3, groups - 1)),
            dma((2, 2, parts)),
            dma((2, 2, parts)),
            dma((parts, groups - 1)),
            dma((parts, groups - 1)),
        ],
        compiler_params=pltpu.CompilerParams(
            collective_id=0, has_side_effects=True, vmem_limit_bytes=48 * 1024 * 1024
        ),
        cost_estimate=pl.CostEstimate(
            flops=12 * height * height * modes,
            bytes_accessed=16 * rows * total + 4 * height * height,
            transcendentals=0,
        ),
    )(
        provisional,
        implicit_terms,
        adv_speed,
        reaction,
        wall_rate[None],
        span_rate[None],
        analysis,
        synthesis,
    )
    return result.astype(f32)[None]


def solution(mesh):
    placed = (
        P(None, "gx", "gy", None),
        P(None, "gx", "gy", None),
        P("gx", None),
        P("gx", None),
        P(),
        P(),
        P(),
        P(),
    )
    return jax.shard_map(
        per_device, mesh=mesh, in_specs=placed, out_specs=P("gx", "gy", None), check_vma=False
    )
```

```python
import functools
import math

import jax
import jax.numpy as jnp
from jax import lax
from jax.experimental import pallas as pl
from jax.experimental.pallas import tpu as pltpu
from jax.sharding import PartitionSpec as P

TILE = 64
BLOCK = 256
PARTS = 2
EARLY = True


def spectral_weights():
    root_five = math.sqrt(5.0)
    points = [0.0, 0.5 - 0.5 / root_five, 0.5 + 0.5 / root_five, 1.0]
    gauss_offset = 1.0 / math.sqrt(3.0)
    weights = [[0.0, 0.0, 0.0, 0.0] for m in range(3)]
    for m in range(3):
        half_width = 0.5 * (points[m + 1] - points[m])
        centre = 0.5 * (points[m + 1] + points[m])
        for sign_factor in (-1.0, 1.0):
            sample = centre + half_width * sign_factor * gauss_offset
            for j in range(4):
                basis_value = 1.0
                for i in range(4):
                    if i != j:
                        basis_value = basis_value * (sample - points[i]) / (points[j] - points[i])
                weights[m][j] = weights[m][j] + half_width * basis_value
    return (points, weights)


def sweep_kernel(
    planes,
    groups,
    parts,
    prov_hbm,
    impl_hbm,
    speed_hbm,
    reaction_hbm,
    wall_hbm,
    span_hbm,
    ana_hbm,
    syn_hbm,
    out_ref,
    lines,
    prov,
    impl,
    ana,
    syn,
    cols,
    mixed,
    mixed_recv,
    local,
    known_send,
    known,
    current,
    rounded,
    scaled,
    sent,
    sent_recv,
    final,
    load_sem,
    mixed_sem,
    mixed_recv_sem,
    known_sem,
    known_recv_sem,
    sent_sem,
    sent_recv_sem,
    final_sem,
    final_recv_sem,
):
    f32, bf16 = jnp.float32, jnp.bfloat16
    rows, modes = prov.shape[1], known.shape[2]
    height = rows * groups
    width = modes // parts
    points, weights = spectral_weights()
    steps = [float(points[m + 1] - points[m]) for m in range(3)]
    gx, me = lax.axis_index("gx"), lax.axis_index("gy")
    sides = (lax.rem(gx + 1, planes), lax.rem(gx + planes - 1, planes))
    row_start = pl.multiple_of(me * rows, rows)
    order = list(range(1, groups)) + [0]

    loads = []
    for j in range(4):
        loads.append(pltpu.make_async_copy(prov_hbm.at[j, 0], prov.at[j], load_sem.at[j]))
    for j in range(4):
        loads.append(pltpu.make_async_copy(impl_hbm.at[j, 0], impl.at[j], load_sem.at[4 + j]))
    loads.append(pltpu.make_async_copy(ana_hbm, ana, load_sem.at[8]))
    loads.append(pltpu.make_async_copy(syn_hbm, syn, load_sem.at[9]))
    for k, ref in enumerate((speed_hbm, reaction_hbm, wall_hbm, span_hbm)):
        loads.append(pltpu.make_async_copy(ref, lines.at[k], load_sem.at[10 + k]))
    for load in loads:
        load.start()

    barrier = pltpu.get_barrier_semaphore()
    for side in sides:
        pl.semaphore_signal(
            barrier, inc=1, device_id=(side, me), device_id_type=pl.DeviceIdType.MESH
        )
    for s in range(1, groups):
        pl.semaphore_signal(
            barrier,
            inc=1,
            device_id=(gx, lax.rem(me + s, groups)),
            device_id_type=pl.DeviceIdType.MESH,
        )

    def over(total, tile, body):
        def step(i, carry):
            body(pl.multiple_of(i * tile, tile))
            return carry

        lax.fori_loop(0, total // tile, step, 0)

    def lanes_of(s):
        return pl.ds(pl.multiple_of(lax.rem(me + s, groups) * modes, modes), modes)

    def remote(src, dst, send, recv, where):
        return pltpu.make_async_remote_copy(
            src_ref=src,
            dst_ref=dst,
            send_sem=send,
            recv_sem=recv,
            device_id=where,
            device_id_type=pl.DeviceIdType.MESH,
        )

    def make_columns():
        for k in range(3):
            for i in range(height // 128):
                line = lines[k, 0:1, i * 128 : (i + 1) * 128] * (0.5 if k == 0 else 1.0)
                block = jnp.broadcast_to(line, (128, 128)).T
                for lane in range(modes // 128):
                    cols[k, i * 128 : (i + 1) * 128, lane * 128 : (lane + 1) * 128] = block

    def mix(m, r, lanes):
        total = None
        for j in range(4):
            weight = float(weights[m][j] - (steps[m] if m == j and m > 0 else 0.0))
            term = weight * prov[j, pl.ds(r, TILE), lanes].astype(f32)
            total = term if total is None else total + term
        return total

    mixed_copies, known_copies, sent_copies, final_copies = {}, {}, {}, {}

    def send_known(m, s):
        copy = remote(
            known_send.at[m, s - 1],
            known.at[m, pl.ds(row_start, rows)],
            known_sem.at[m, s - 1],
            known_recv_sem.at[m, s - 1],
            (gx, lax.rem(me + s, groups)),
        )
        copy.start()
        known_copies[m, s] = copy

    def make_mixed(m, s):
        lanes = lanes_of(s)

        def body(r):
            value = mix(m, r, lanes).astype(bf16)
            if m < 2:
                mixed[m, s, pl.ds(r, TILE), :] = value
            elif s:
                known_send[3, s - 1, pl.ds(r, TILE), :] = value
            else:
                known[3, pl.ds(pl.multiple_of(row_start + r, TILE), TILE), :] = value

        over(rows, TILE, body)
        if m == 2 and s:
            send_known(3, s)

    def make_local(m, s):
        lanes = lanes_of(s)

        def body(r):
            here = pl.ds(pl.multiple_of(row_start + r, TILE), TILE)
            total = -cols[1, here, :] * mix(m, r, lanes)
            if m == 0:
                total = total + prov[0, pl.ds(r, TILE), lanes].astype(f32)
            for j in range(4):
                weight = float(weights[m][j] - (steps[m] if j == m + 1 else 0.0))
                total = total + weight * impl[j, pl.ds(r, TILE), lanes].astype(f32)
            local[m, s, pl.ds(r, TILE), :] = total

        over(rows, TILE, body)

    def send_mixed(m, s):
        for d in range(2):
            copy = remote(
                mixed.at[m, s],
                mixed_recv.at[m, d, s],
                mixed_sem.at[m, d, s],
                mixed_recv_sem.at[m, d, s],
                (sides[d], me),
            )
            copy.start()
            mixed_copies[m, d, s] = copy

    def make_known(m, s):
        if m < 2:
            for d in range(2):
                mixed_copies[m, d, s].wait_recv()

        def body(r):
            here = pl.ds(pl.multiple_of(row_start + r, TILE), TILE)
            value = local[m, s, pl.ds(r, TILE), :]
            if m < 2:
                ahead = mixed_recv[m, 1, s, pl.ds(r, TILE), :].astype(f32)
                behind = mixed_recv[m, 0, s, pl.ds(r, TILE), :].astype(f32)
                value = value - cols[0, here, :] * (ahead - behind)
            if s:
                known_send[m, s - 1, pl.ds(r, TILE), :] = value.astype(bf16)
            else:
                known[m, here, :] = value.astype(bf16)

        over(rows, TILE, body)
        if s:
            send_known(m, s)

    def solve(m, p):
        span = lines[3, 0:1, pl.ds(pl.multiple_of(me * modes + p * width, width), width)]
        part = slice(p * width, (p + 1) * width)

        def make_rhs(r):
            here = pl.ds(r, TILE)
            rhs = known[m, here, part].astype(f32)
            if m:
                ahead = sent_recv[m - 1, 1, p, here, :].astype(f32)
                behind = sent_recv[m - 1, 0, p, here, :].astype(f32)
                change = cols[0, here, part] * (ahead - behind)
                if m == 1:
                    change = steps[m] * change
                rhs = rhs + current[p, here, :] - change
            rounded[p, here, :] = rhs.astype(bf16)

        over(height, TILE, make_rhs)

        def to_modes(r):
            here = pl.ds(r, BLOCK)
            factors = 1.0 / (1.0 + steps[m] * (cols[2, here, part] + span))
            coefficients = jnp.dot(ana[here, :], rounded[p], preferred_element_type=f32)
            scaled[p, here, :] = (coefficients * factors).astype(bf16)

        over(height, BLOCK, to_modes)

        def to_points(r):
            here = pl.ds(r, BLOCK)
            value = jnp.dot(syn[here, :], scaled[p], preferred_element_type=f32)
            if m < 2:
                own = value.astype(bf16).astype(f32)
                current[p, here, :] = value - steps[m + 1] * cols[1, here, part] * own
                if m == 1:
                    own = steps[m + 1] * own + known[3, here, part].astype(f32)
                sent[m, p, here, :] = own.astype(bf16)
            else:
                final[p, here, :] = value.astype(bf16)

        over(height, BLOCK, to_points)
        if m < 2:
            for d in range(2):
                copy = remote(
                    sent.at[m, p],
                    sent_recv.at[m, d, p],
                    sent_sem.at[m, d, p],
                    sent_recv_sem.at[m, d, p],
                    (sides[d], me),
                )
                copy.start()
                sent_copies[m, d, p] = copy
        else:
            own = pl.ds(pl.multiple_of(me * modes + p * width, width), width)
            for s in range(1, groups):
                other = lax.rem(me + s, groups)
                copy = remote(
                    final.at[p, pl.ds(pl.multiple_of(other * rows, rows), rows)],
                    out_ref.at[:, own],
                    final_sem.at[p, s - 1],
                    final_recv_sem.at[p, s - 1],
                    (gx, other),
                )
                copy.start()
                final_copies[p, s] = copy
            out_ref[:, own] = final[p, pl.ds(row_start, rows), :]

    for load in loads[:4]:
        load.wait()
    for s in order:
        make_mixed(0, s)
        if s == order[0]:
            pl.semaphore_wait(barrier, 2 + groups - 1)
        send_mixed(0, s)
    for load in loads[10:]:
        load.wait()
    make_columns()
    for load in loads[4:8]:
        load.wait()
    for s in order:
        make_local(0, s)
    if EARLY:
        for s in order:
            make_mixed(2, s)
    for s in order:
        make_known(0, s)
        make_mixed(1, s)
        send_mixed(1, s)
    for m in (1, 2):
        for s in order:
            make_local(m, s)
    for load in loads[8:10]:
        load.wait()
    for m in range(3):
        for s in range(1, groups):
            known_copies[m, s].wait_recv()
            if m == 1:
                known_copies[3, s].wait_recv()
        for p in range(parts):
            if m:
                for d in range(2):
                    sent_copies[m - 1, d, p].wait_recv()
            solve(m, p)
        if m == 0:
            for s in order:
                make_known(1, s)
            if not EARLY:
                for s in order:
                    make_mixed(2, s)
            for s in order:
                make_known(2, s)
    for copy in final_copies.values():
        copy.wait_recv()
    for group in (mixed_copies, known_copies, sent_copies, final_copies):
        for copy in group.values():
            copy.wait_send()


def per_device(
    provisional, implicit_terms, adv_speed, reaction, wall_rate, span_rate, analysis, synthesis
):
    planes, groups = lax.axis_size("gx"), lax.axis_size("gy")
    rows, total = provisional.shape[2], provisional.shape[3]
    height, modes = rows * groups, total // groups
    parts = max(1, min(PARTS, modes // 128))
    width = modes // parts
    f32, bf16 = jnp.float32, jnp.bfloat16
    dma = pltpu.SemaphoreType.DMA
    vmem = pl.BlockSpec(memory_space=pltpu.VMEM)
    hbm = pl.BlockSpec(memory_space=pl.ANY)
    result = pl.pallas_call(
        functools.partial(sweep_kernel, planes, groups, parts),
        out_shape=jax.ShapeDtypeStruct((rows, total), bf16),
        in_specs=[hbm] * 8,
        out_specs=vmem,
        scratch_shapes=[
            pltpu.VMEM((4, 1, height), f32),
            pltpu.VMEM((4, rows, total), bf16),
            pltpu.VMEM((4, rows, total), bf16),
            pltpu.VMEM((height, height), bf16),
            pltpu.VMEM((height, height), bf16),
            pltpu.VMEM((3, height, modes), f32),
            pltpu.VMEM((2, groups, rows, modes), bf16),
            pltpu.VMEM((2, 2, groups, rows, modes), bf16),
            pltpu.VMEM((3, groups, rows, modes), f32),
            pltpu.VMEM((4, groups - 1, rows, modes), bf16),
            pltpu.VMEM((4, height, modes), bf16),
            pltpu.VMEM((parts, height, width), f32),
            pltpu.VMEM((parts, height, width), bf16),
            pltpu.VMEM((parts, height, width), bf16),
            pltpu.VMEM((2, parts, height, width), bf16),
            pltpu.VMEM((2, 2, parts, height, width), bf16),
            pltpu.VMEM((parts, height, width), bf16),
            dma((14,)),
            dma((2, 2, groups)),
            dma((2, 2, groups)),
            dma((4, groups - 1)),
            dma((4, groups - 1)),
            dma((2, 2, parts)),
            dma((2, 2, parts)),
            dma((parts, groups - 1)),
            dma((parts, groups - 1)),
        ],
        compiler_params=pltpu.CompilerParams(
            collective_id=0, has_side_effects=True, vmem_limit_bytes=60 * 1024 * 1024
        ),
        cost_estimate=pl.CostEstimate(
            flops=12 * height * height * modes,
            bytes_accessed=16 * rows * total + 4 * height * height,
            transcendentals=0,
        ),
    )(
        provisional,
        implicit_terms,
        adv_speed,
        reaction,
        wall_rate[None],
        span_rate[None],
        analysis,
        synthesis,
    )
    return result.astype(f32)[None]


def solution(mesh):
    placed = (
        P(None, "gx", "gy", None),
        P(None, "gx", "gy", None),
        P("gx", None),
        P("gx", None),
        P(),
        P(),
        P(),
        P(),
    )
    return jax.shard_map(
        per_device, mesh=mesh, in_specs=placed, out_specs=P("gx", "gy", None), check_vma=False
    )
```

```python
import functools
import math

import jax
import jax.numpy as jnp
from jax import lax
from jax.experimental import pallas as pl
from jax.experimental.pallas import tpu as pltpu
from jax.sharding import PartitionSpec as P

TILE = 64
BLOCK = 256
PARTS = 2


def spectral_weights():
    root_five = math.sqrt(5.0)
    points = [0.0, 0.5 - 0.5 / root_five, 0.5 + 0.5 / root_five, 1.0]
    gauss_offset = 1.0 / math.sqrt(3.0)
    weights = [[0.0, 0.0, 0.0, 0.0] for m in range(3)]
    for m in range(3):
        half_width = 0.5 * (points[m + 1] - points[m])
        centre = 0.5 * (points[m + 1] + points[m])
        for sign_factor in (-1.0, 1.0):
            sample = centre + half_width * sign_factor * gauss_offset
            for j in range(4):
                basis_value = 1.0
                for i in range(4):
                    if i != j:
                        basis_value = basis_value * (sample - points[i]) / (points[j] - points[i])
                weights[m][j] = weights[m][j] + half_width * basis_value
    return (points, weights)


def sweep_kernel(
    planes,
    groups,
    parts,
    prov_hbm,
    impl_hbm,
    speed_hbm,
    reaction_hbm,
    wall_hbm,
    span_hbm,
    ana_hbm,
    syn_hbm,
    out_ref,
    lines,
    prov,
    impl,
    ana,
    syn,
    cols,
    mixed,
    mixed_recv,
    local,
    known_send,
    known,
    current,
    rounded,
    scaled,
    sent,
    sent_recv,
    final,
    load_sem,
    mixed_sem,
    mixed_recv_sem,
    known_sem,
    known_recv_sem,
    sent_sem,
    sent_recv_sem,
    final_sem,
    final_recv_sem,
):
    f32, bf16 = jnp.float32, jnp.bfloat16
    rows, modes = prov.shape[1], mixed.shape[3]
    height = rows * groups
    width = modes // parts
    points, weights = spectral_weights()
    steps = [float(points[m + 1] - points[m]) for m in range(3)]
    gx, me = lax.axis_index("gx"), lax.axis_index("gy")
    sides = (lax.rem(gx + 1, planes), lax.rem(gx + planes - 1, planes))
    row_start = pl.multiple_of(me * rows, rows)
    order = [2, 1, 3, 0] if groups == 4 else list(range(1, groups)) + [0]

    loads = []
    for j in range(4):
        loads.append(pltpu.make_async_copy(prov_hbm.at[j, 0], prov.at[j], load_sem.at[j]))
    for j in range(4):
        loads.append(pltpu.make_async_copy(impl_hbm.at[j, 0], impl.at[j], load_sem.at[4 + j]))
    loads.append(pltpu.make_async_copy(ana_hbm, ana, load_sem.at[8]))
    loads.append(pltpu.make_async_copy(syn_hbm, syn, load_sem.at[9]))
    for k, ref in enumerate((speed_hbm, reaction_hbm, wall_hbm, span_hbm)):
        loads.append(pltpu.make_async_copy(ref, lines.at[k], load_sem.at[10 + k]))
    for load in loads:
        load.start()

    barrier = pltpu.get_barrier_semaphore()
    for side in sides:
        pl.semaphore_signal(
            barrier, inc=1, device_id=(side, me), device_id_type=pl.DeviceIdType.MESH
        )
    for s in range(1, groups):
        pl.semaphore_signal(
            barrier,
            inc=1,
            device_id=(gx, lax.rem(me + s, groups)),
            device_id_type=pl.DeviceIdType.MESH,
        )

    def over(total, tile, body):
        def step(i, carry):
            body(pl.multiple_of(i * tile, tile))
            return carry

        lax.fori_loop(0, total // tile, step, 0)

    def lanes_of(s):
        return pl.ds(pl.multiple_of(lax.rem(me + s, groups) * modes, modes), modes)

    def remote(src, dst, send, recv, where):
        return pltpu.make_async_remote_copy(
            src_ref=src,
            dst_ref=dst,
            send_sem=send,
            recv_sem=recv,
            device_id=where,
            device_id_type=pl.DeviceIdType.MESH,
        )

    def make_columns():
        for k in range(3):
            for i in range(height // 128):
                line = lines[k, 0:1, i * 128 : (i + 1) * 128] * (0.5 if k == 0 else 1.0)
                block = jnp.broadcast_to(line, (128, 128)).T
                for lane in range(modes // 128):
                    cols[k, i * 128 : (i + 1) * 128, lane * 128 : (lane + 1) * 128] = block

    def mix(m, r, lanes):
        total = None
        for j in range(4):
            weight = float(weights[m][j] - (steps[m] if m == j and m > 0 else 0.0))
            term = weight * prov[j, pl.ds(r, TILE), lanes].astype(f32)
            total = term if total is None else total + term
        return total

    def make_mixed(m, s):
        lanes = lanes_of(s)

        def body(r):
            mixed[m, s, pl.ds(r, TILE), :] = mix(m, r, lanes).astype(bf16)

        over(rows, TILE, body)

    def make_local(m, s):
        lanes = lanes_of(s)

        def body(r):
            here = pl.ds(pl.multiple_of(row_start + r, TILE), TILE)
            total = -cols[1, here, :] * mix(m, r, lanes)
            if m == 0:
                total = total + prov[0, pl.ds(r, TILE), lanes].astype(f32)
            for j in range(4):
                weight = float(weights[m][j] - (steps[m] if j == m + 1 else 0.0))
                total = total + weight * impl[j, pl.ds(r, TILE), lanes].astype(f32)
            local[m, s, pl.ds(r, TILE), :] = total

        over(rows, TILE, body)

    mixed_copies, known_copies, sent_copies, final_copies = {}, {}, {}, {}

    def send_mixed(m, s):
        for d in range(2):
            copy = remote(
                mixed.at[m, s],
                mixed_recv.at[m, d, s],
                mixed_sem.at[m, d, s],
                mixed_recv_sem.at[m, d, s],
                (sides[d], me),
            )
            copy.start()
            mixed_copies[m, d, s] = copy

    def make_known(m, s):
        for d in range(2):
            mixed_copies[m, d, s].wait_recv()

        def body(r):
            here = pl.ds(pl.multiple_of(row_start + r, TILE), TILE)
            ahead = mixed_recv[m, 1, s, pl.ds(r, TILE), :].astype(f32)
            behind = mixed_recv[m, 0, s, pl.ds(r, TILE), :].astype(f32)
            value = local[m, s, pl.ds(r, TILE), :] - cols[0, here, :] * (ahead - behind)
            value = value.astype(bf16)
            for p in range(parts):
                part = slice(p * width, (p + 1) * width)
                if s:
                    known_send[m, s - 1, p, pl.ds(r, TILE), :] = value[:, part]
                else:
                    known[m, p, here, :] = value[:, part]

        over(rows, TILE, body)

    def send_known(m, s, p):
        if s:
            copy = remote(
                known_send.at[m, s - 1, p],
                known.at[m, p, pl.ds(row_start, rows)],
                known_sem.at[m, s - 1, p],
                known_recv_sem.at[m, s - 1, p],
                (gx, lax.rem(me + s, groups)),
            )
            copy.start()
            known_copies[m, s, p] = copy

    def solve(m, p):
        span = lines[3, 0:1, pl.ds(pl.multiple_of(me * modes + p * width, width), width)]
        part = slice(p * width, (p + 1) * width)

        def make_rhs(r):
            here = pl.ds(r, TILE)
            rhs = known[m, p, here, :].astype(f32)
            if m:
                ahead = sent_recv[m - 1, 1, p, here, :].astype(f32)
                behind = sent_recv[m - 1, 0, p, here, :].astype(f32)
                own = sent[m - 1, p, here, :].astype(f32)
                rhs = (
                    rhs
                    + current[p, here, :]
                    - steps[m]
                    * (cols[1, here, part] * own + cols[0, here, part] * (ahead - behind))
                )
            rounded[p, here, :] = rhs.astype(bf16)

        over(height, TILE, make_rhs)

        def to_modes(r):
            here = pl.ds(r, BLOCK)
            factors = 1.0 / (1.0 + steps[m] * (cols[2, here, part] + span))
            coefficients = jnp.dot(ana[here, :], rounded[p], preferred_element_type=f32)
            scaled[p, here, :] = (coefficients * factors).astype(bf16)

        over(height, BLOCK, to_modes)

        def to_points(r):
            here = pl.ds(r, BLOCK)
            value = jnp.dot(syn[here, :], scaled[p], preferred_element_type=f32)
            if m < 2:
                current[p, here, :] = value
                sent[m, p, here, :] = value.astype(bf16)
            else:
                final[p, here, :] = value.astype(bf16)

        over(height, BLOCK, to_points)
        if m < 2:
            for d in range(2):
                copy = remote(
                    sent.at[m, p],
                    sent_recv.at[m, d, p],
                    sent_sem.at[m, d, p],
                    sent_recv_sem.at[m, d, p],
                    (sides[d], me),
                )
                copy.start()
                sent_copies[m, d, p] = copy
        else:
            own = pl.ds(pl.multiple_of(me * modes + p * width, width), width)
            for s in range(1, groups):
                other = lax.rem(me + s, groups)
                copy = remote(
                    final.at[p, pl.ds(pl.multiple_of(other * rows, rows), rows)],
                    out_ref.at[:, own],
                    final_sem.at[p, s - 1],
                    final_recv_sem.at[p, s - 1],
                    (gx, other),
                )
                copy.start()
                final_copies[p, s] = copy
            out_ref[:, own] = final[p, pl.ds(row_start, rows), :]

    for load in loads[:4]:
        load.wait()
    for s in order:
        make_mixed(0, s)
        if s == order[0]:
            pl.semaphore_wait(barrier, 2 + groups - 1)
        send_mixed(0, s)
    for load in loads[10:]:
        load.wait()
    make_columns()
    for load in loads[4:8]:
        load.wait()
    for s in order:
        make_local(0, s)
    def build(m):
        if m < 2:
            for s in order:
                make_mixed(m + 1, s)
        for s in order:
            if m:
                make_local(m, s)
            make_known(m, s)
            if m == 0:
                for p in range(parts):
                    send_known(0, s, p)
            if m < 2:
                send_mixed(m + 1, s)

    build(0)
    build(1)
    for load in loads[8:10]:
        load.wait()
    for m in range(3):
        for p in range(parts):
            for s in range(1, groups):
                known_copies[m, s, p].wait_recv()
            if m < 2:
                for s in order:
                    send_known(m + 1, s, p)
            if m:
                for d in range(2):
                    sent_copies[m - 1, d, p].wait_recv()
            solve(m, p)
        if m == 0:
            build(2)
    for copy in final_copies.values():
        copy.wait_recv()
    for group in (mixed_copies, known_copies, sent_copies, final_copies):
        for copy in group.values():
            copy.wait_send()


def per_device(
    provisional, implicit_terms, adv_speed, reaction, wall_rate, span_rate, analysis, synthesis
):
    planes, groups = lax.axis_size("gx"), lax.axis_size("gy")
    rows, total = provisional.shape[2], provisional.shape[3]
    height, modes = rows * groups, total // groups
    parts = max(1, min(PARTS, modes // 128))
    width = modes // parts
    f32, bf16 = jnp.float32, jnp.bfloat16
    dma = pltpu.SemaphoreType.DMA
    vmem = pl.BlockSpec(memory_space=pltpu.VMEM)
    hbm = pl.BlockSpec(memory_space=pl.ANY)
    result = pl.pallas_call(
        functools.partial(sweep_kernel, planes, groups, parts),
        out_shape=jax.ShapeDtypeStruct((rows, total), bf16),
        in_specs=[hbm] * 8,
        out_specs=vmem,
        scratch_shapes=[
            pltpu.VMEM((4, 1, height), f32),
            pltpu.VMEM((4, rows, total), bf16),
            pltpu.VMEM((4, rows, total), bf16),
            pltpu.VMEM((height, height), bf16),
            pltpu.VMEM((height, height), bf16),
            pltpu.VMEM((3, height, modes), f32),
            pltpu.VMEM((3, groups, rows, modes), bf16),
            pltpu.VMEM((3, 2, groups, rows, modes), bf16),
            pltpu.VMEM((3, groups, rows, modes), f32),
            pltpu.VMEM((3, groups - 1, parts, rows, width), bf16),
            pltpu.VMEM((3, parts, height, width), bf16),
            pltpu.VMEM((parts, height, width), f32),
            pltpu.VMEM((parts, height, width), bf16),
            pltpu.VMEM((parts, height, width), bf16),
            pltpu.VMEM((2, parts, height, width), bf16),
            pltpu.VMEM((2, 2, parts, height, width), bf16),
            pltpu.VMEM((parts, height, width), bf16),
            dma((14,)),
            dma((3, 2, groups)),
            dma((3, 2, groups)),
            dma((3, groups - 1, parts)),
            dma((3, groups - 1, parts)),
            dma((2, 2, parts)),
            dma((2, 2, parts)),
            dma((parts, groups - 1)),
            dma((parts, groups - 1)),
        ],
        compiler_params=pltpu.CompilerParams(
            collective_id=0, has_side_effects=True, vmem_limit_bytes=60 * 1024 * 1024
        ),
        cost_estimate=pl.CostEstimate(
            flops=12 * height * height * modes,
            bytes_accessed=16 * rows * total + 4 * height * height,
            transcendentals=0,
        ),
    )(
        provisional,
        implicit_terms,
        adv_speed,
        reaction,
        wall_rate[None],
        span_rate[None],
        analysis,
        synthesis,
    )
    return result.astype(f32)[None]


def solution(mesh):
    placed = (
        P(None, "gx", "gy", None),
        P(None, "gx", "gy", None),
        P("gx", None),
        P("gx", None),
        P(),
        P(),
        P(),
        P(),
    )
    return jax.shard_map(
        per_device, mesh=mesh, in_specs=placed, out_specs=P("gx", "gy", None), check_vma=False
    )
```

```python
import functools
import math

import jax
import jax.numpy as jnp
from jax import lax
from jax.experimental import pallas as pl
from jax.experimental.pallas import tpu as pltpu
from jax.sharding import PartitionSpec as P

TILE = 64
BLOCK = 512
PARTS = 2


def spectral_weights():
    root_five = math.sqrt(5.0)
    points = [0.0, 0.5 - 0.5 / root_five, 0.5 + 0.5 / root_five, 1.0]
    gauss_offset = 1.0 / math.sqrt(3.0)
    weights = [[0.0, 0.0, 0.0, 0.0] for m in range(3)]
    for m in range(3):
        half_width = 0.5 * (points[m + 1] - points[m])
        centre = 0.5 * (points[m + 1] + points[m])
        for sign_factor in (-1.0, 1.0):
            sample = centre + half_width * sign_factor * gauss_offset
            for j in range(4):
                basis_value = 1.0
                for i in range(4):
                    if i != j:
                        basis_value = basis_value * (sample - points[i]) / (points[j] - points[i])
                weights[m][j] = weights[m][j] + half_width * basis_value
    return (points, weights)


def sweep_kernel(
    planes,
    groups,
    parts,
    prov_hbm,
    impl_hbm,
    speed_hbm,
    reaction_hbm,
    wall_hbm,
    span_hbm,
    ana_hbm,
    syn_hbm,
    out_ref,
    lines,
    prov,
    impl,
    ana,
    syn,
    cols,
    mixed,
    mixed_recv,
    local,
    known_send,
    known,
    current,
    rounded,
    scaled,
    sent,
    sent_recv,
    final,
    load_sem,
    mixed_sem,
    mixed_recv_sem,
    known_sem,
    known_recv_sem,
    sent_sem,
    sent_recv_sem,
    final_sem,
    final_recv_sem,
):
    f32, bf16 = jnp.float32, jnp.bfloat16
    rows, modes = prov.shape[1], mixed.shape[3]
    height = rows * groups
    width = modes // parts
    points, weights = spectral_weights()
    steps = [float(points[m + 1] - points[m]) for m in range(3)]
    gx, me = lax.axis_index("gx"), lax.axis_index("gy")
    sides = (lax.rem(gx + 1, planes), lax.rem(gx + planes - 1, planes))
    row_start = pl.multiple_of(me * rows, rows)
    order = [2, 1, 3, 0] if groups == 4 else list(range(1, groups)) + [0]

    loads = []
    for j in range(4):
        loads.append(pltpu.make_async_copy(prov_hbm.at[j, 0], prov.at[j], load_sem.at[j]))
    for j in range(4):
        loads.append(pltpu.make_async_copy(impl_hbm.at[j, 0], impl.at[j], load_sem.at[4 + j]))
    loads.append(pltpu.make_async_copy(ana_hbm, ana, load_sem.at[8]))
    loads.append(pltpu.make_async_copy(syn_hbm, syn, load_sem.at[9]))
    for k, ref in enumerate((speed_hbm, reaction_hbm, wall_hbm, span_hbm)):
        loads.append(pltpu.make_async_copy(ref, lines.at[k], load_sem.at[10 + k]))
    for load in loads:
        load.start()

    barrier = pltpu.get_barrier_semaphore()
    for side in sides:
        pl.semaphore_signal(
            barrier, inc=1, device_id=(side, me), device_id_type=pl.DeviceIdType.MESH
        )
    for s in range(1, groups):
        pl.semaphore_signal(
            barrier,
            inc=1,
            device_id=(gx, lax.rem(me + s, groups)),
            device_id_type=pl.DeviceIdType.MESH,
        )

    def over(total, tile, body):
        def step(i, carry):
            body(pl.multiple_of(i * tile, tile))
            return carry

        lax.fori_loop(0, total // tile, step, 0)

    def lanes_of(s):
        return pl.ds(pl.multiple_of(lax.rem(me + s, groups) * modes, modes), modes)

    def remote(src, dst, send, recv, where):
        return pltpu.make_async_remote_copy(
            src_ref=src,
            dst_ref=dst,
            send_sem=send,
            recv_sem=recv,
            device_id=where,
            device_id_type=pl.DeviceIdType.MESH,
        )

    def make_columns():
        for k in range(3):
            for i in range(height // 128):
                line = lines[k, 0:1, i * 128 : (i + 1) * 128] * (0.5 if k == 0 else 1.0)
                block = jnp.broadcast_to(line, (128, 128)).T
                for lane in range(modes // 128):
                    cols[k, i * 128 : (i + 1) * 128, lane * 128 : (lane + 1) * 128] = block

    def mix(m, r, lanes):
        total = None
        for j in range(4):
            weight = float(weights[m][j] - (steps[m] if m == j and m > 0 else 0.0))
            term = weight * prov[j, pl.ds(r, TILE), lanes].astype(f32)
            total = term if total is None else total + term
        return total

    def make_mixed(m, s):
        lanes = lanes_of(s)

        def body(r):
            mixed[m, s, pl.ds(r, TILE), :] = mix(m, r, lanes).astype(bf16)

        over(rows, TILE, body)

    def make_local(m, s):
        lanes = lanes_of(s)

        def body(r):
            here = pl.ds(pl.multiple_of(row_start + r, TILE), TILE)
            total = -cols[1, here, :] * mix(m, r, lanes)
            if m == 0:
                total = total + prov[0, pl.ds(r, TILE), lanes].astype(f32)
            for j in range(4):
                weight = float(weights[m][j] - (steps[m] if j == m + 1 else 0.0))
                total = total + weight * impl[j, pl.ds(r, TILE), lanes].astype(f32)
            local[m, s, pl.ds(r, TILE), :] = total

        over(rows, TILE, body)

    mixed_copies, known_copies, sent_copies, final_copies = {}, {}, {}, {}

    def send_mixed(m, s):
        for d in range(2):
            copy = remote(
                mixed.at[m, s],
                mixed_recv.at[m, d, s],
                mixed_sem.at[m, d, s],
                mixed_recv_sem.at[m, d, s],
                (sides[d], me),
            )
            copy.start()
            mixed_copies[m, d, s] = copy

    def make_known(m, s):
        for d in range(2):
            mixed_copies[m, d, s].wait_recv()

        def body(r):
            here = pl.ds(pl.multiple_of(row_start + r, TILE), TILE)
            ahead = mixed_recv[m, 1, s, pl.ds(r, TILE), :].astype(f32)
            behind = mixed_recv[m, 0, s, pl.ds(r, TILE), :].astype(f32)
            value = local[m, s, pl.ds(r, TILE), :] - cols[0, here, :] * (ahead - behind)
            value = value.astype(bf16)
            for p in range(parts):
                part = slice(p * width, (p + 1) * width)
                if s:
                    known_send[m, s - 1, p, pl.ds(r, TILE), :] = value[:, part]
                else:
                    known[m, p, here, :] = value[:, part]

        over(rows, TILE, body)

    def send_known(m, s, p):
        if s:
            copy = remote(
                known_send.at[m, s - 1, p],
                known.at[m, p, pl.ds(row_start, rows)],
                known_sem.at[m, s - 1, p],
                known_recv_sem.at[m, s - 1, p],
                (gx, lax.rem(me + s, groups)),
            )
            copy.start()
            known_copies[m, s, p] = copy

    def solve(m, p):
        span = lines[3, 0:1, pl.ds(pl.multiple_of(me * modes + p * width, width), width)]
        part = slice(p * width, (p + 1) * width)

        def make_rhs(r):
            here = pl.ds(r, TILE)
            rhs = known[m, p, here, :].astype(f32)
            if m:
                ahead = sent_recv[m - 1, 1, p, here, :].astype(f32)
                behind = sent_recv[m - 1, 0, p, here, :].astype(f32)
                own = sent[m - 1, p, here, :].astype(f32)
                rhs = (
                    rhs
                    + current[p, here, :]
                    - steps[m]
                    * (cols[1, here, part] * own + cols[0, here, part] * (ahead - behind))
                )
            rounded[p, here, :] = rhs.astype(bf16)

        over(height, TILE, make_rhs)

        def to_modes(r):
            here = pl.ds(r, BLOCK)
            factors = 1.0 / (1.0 + steps[m] * (cols[2, here, part] + span))
            coefficients = jnp.dot(ana[here, :], rounded[p], preferred_element_type=f32)
            scaled[p, here, :] = (coefficients * factors).astype(bf16)

        over(height, BLOCK, to_modes)

        def to_points(r):
            here = pl.ds(r, BLOCK)
            value = jnp.dot(syn[here, :], scaled[p], preferred_element_type=f32)
            if m < 2:
                current[p, here, :] = value
                sent[m, p, here, :] = value.astype(bf16)
            else:
                final[p, here, :] = value.astype(bf16)

        over(height, BLOCK, to_points)
        if m < 2:
            for d in range(2):
                copy = remote(
                    sent.at[m, p],
                    sent_recv.at[m, d, p],
                    sent_sem.at[m, d, p],
                    sent_recv_sem.at[m, d, p],
                    (sides[d], me),
                )
                copy.start()
                sent_copies[m, d, p] = copy
        else:
            own = pl.ds(pl.multiple_of(me * modes + p * width, width), width)
            for s in order[:-1]:
                other = lax.rem(me + s, groups)
                copy = remote(
                    final.at[p, pl.ds(pl.multiple_of(other * rows, rows), rows)],
                    out_ref.at[:, own],
                    final_sem.at[p, s - 1],
                    final_recv_sem.at[p, s - 1],
                    (gx, other),
                )
                copy.start()
                final_copies[p, s] = copy
            out_ref[:, own] = final[p, pl.ds(row_start, rows), :]

    for load in loads[:4]:
        load.wait()
    for s in order:
        make_mixed(0, s)
        if s == order[0]:
            pl.semaphore_wait(barrier, 2 + groups - 1)
        send_mixed(0, s)
    for load in loads[10:]:
        load.wait()
    make_columns()
    for load in loads[4:8]:
        load.wait()
    for s in order:
        make_local(0, s)
    def build(m):
        if m < 2:
            for s in order:
                make_mixed(m + 1, s)
        for s in order:
            if m:
                make_local(m, s)
            make_known(m, s)
            if m == 0:
                for p in range(parts):
                    send_known(0, s, p)
            if m < 2:
                send_mixed(m + 1, s)

    build(0)
    build(1)
    for load in loads[8:10]:
        load.wait()
    for m in range(3):
        for p in range(parts):
            for s in range(1, groups):
                known_copies[m, s, p].wait_recv()
            if m < 2:
                for s in order:
                    send_known(m + 1, s, p)
            if m:
                for d in range(2):
                    sent_copies[m - 1, d, p].wait_recv()
            solve(m, p)
        if m == 0:
            build(2)
    for copy in final_copies.values():
        copy.wait_recv()
    for group in (mixed_copies, known_copies, sent_copies, final_copies):
        for copy in group.values():
            copy.wait_send()


def per_device(
    provisional, implicit_terms, adv_speed, reaction, wall_rate, span_rate, analysis, synthesis
):
    planes, groups = lax.axis_size("gx"), lax.axis_size("gy")
    rows, total = provisional.shape[2], provisional.shape[3]
    height, modes = rows * groups, total // groups
    parts = max(1, min(PARTS, modes // 128))
    width = modes // parts
    f32, bf16 = jnp.float32, jnp.bfloat16
    dma = pltpu.SemaphoreType.DMA
    vmem = pl.BlockSpec(memory_space=pltpu.VMEM)
    hbm = pl.BlockSpec(memory_space=pl.ANY)
    result = pl.pallas_call(
        functools.partial(sweep_kernel, planes, groups, parts),
        out_shape=jax.ShapeDtypeStruct((rows, total), bf16),
        in_specs=[hbm] * 8,
        out_specs=vmem,
        scratch_shapes=[
            pltpu.VMEM((4, 1, height), f32),
            pltpu.VMEM((4, rows, total), bf16),
            pltpu.VMEM((4, rows, total), bf16),
            pltpu.VMEM((height, height), bf16),
            pltpu.VMEM((height, height), bf16),
            pltpu.VMEM((3, height, modes), f32),
            pltpu.VMEM((3, groups, rows, modes), bf16),
            pltpu.VMEM((3, 2, groups, rows, modes), bf16),
            pltpu.VMEM((3, groups, rows, modes), f32),
            pltpu.VMEM((3, groups - 1, parts, rows, width), bf16),
            pltpu.VMEM((3, parts, height, width), bf16),
            pltpu.VMEM((parts, height, width), f32),
            pltpu.VMEM((parts, height, width), bf16),
            pltpu.VMEM((parts, height, width), bf16),
            pltpu.VMEM((2, parts, height, width), bf16),
            pltpu.VMEM((2, 2, parts, height, width), bf16),
            pltpu.VMEM((parts, height, width), bf16),
            dma((14,)),
            dma((3, 2, groups)),
            dma((3, 2, groups)),
            dma((3, groups - 1, parts)),
            dma((3, groups - 1, parts)),
            dma((2, 2, parts)),
            dma((2, 2, parts)),
            dma((parts, groups - 1)),
            dma((parts, groups - 1)),
        ],
        compiler_params=pltpu.CompilerParams(
            collective_id=0, has_side_effects=True, vmem_limit_bytes=60 * 1024 * 1024
        ),
        cost_estimate=pl.CostEstimate(
            flops=12 * height * height * modes,
            bytes_accessed=16 * rows * total + 4 * height * height,
            transcendentals=0,
        ),
    )(
        provisional,
        implicit_terms,
        adv_speed,
        reaction,
        wall_rate[None],
        span_rate[None],
        analysis,
        synthesis,
    )
    return result.astype(f32)[None]


def solution(mesh):
    placed = (
        P(None, "gx", "gy", None),
        P(None, "gx", "gy", None),
        P("gx", None),
        P("gx", None),
        P(),
        P(),
        P(),
        P(),
    )
    return jax.shard_map(
        per_device, mesh=mesh, in_specs=placed, out_specs=P("gx", "gy", None), check_vma=False
    )
```
